32 devices in a mesh: src: 8 (over z, x), rcv: 4 (over y, core).
Axes of the slice: x: 2, y: 2, z: 4, core: 2. Of those that a mesh axis runs over, the one named last changes fastest.
Arguments:
- raw_samples: bfloat16 [12, 4096, 1024], P('rcv', 'src'), may hold values from -400 to 400
- channel_of_row: int32 [4096], P('src'), may hold values from 0 to 4095, as said below
- live_channels: int32 [4096], P('src'), may hold values 0 or 1
- band_reach: int32 [4096], P('src'), may hold values from 1 to 2047
- bin_taper: float32 [64], replicated, may hold values from 0.5 to 2
Outputs:
- correlations: bfloat16 [4096, 65536], P('src', 'rcv')
The draws below stay inside these ranges and needn't reach their ends.
Inputs may be any that keep to these rules, and one draw needn't show every extreme that they name: `channel_of_row`: rows 512 s to 512 (s + 1) - 1 hold, in some order, each channel c with c % 8 == s once.
All inputs are finite; a program needn't handle non-finite values. No bound on the sum of `live_channels` on one device may be relied on, other than what follows from the above.
Results may differ from the reference program's by a relative error of at most 0.0081.
Values may be sent and summed in bfloat16 or wider, within the bound.
A program may use at most 128 MiB of HBM per device.

```python
import math
import jax
import jax.numpy as jnp
from jax import lax

CHB = 512
L = 1024
F = 64
K0 = 32
HW = 64
LAGS = 32
CH = 4096
W = 12
BAND = 2048
N_SRC = 8
N_RCV = 4


def draw_raw_samples(key, part):
    key_base = jax.random.fold_in(key, 0)
    key_scale = jax.random.fold_in(key, 2)
    key_env = jax.random.fold_in(key, 3)
    base = jax.random.normal(key_base, (W, CH, L), jnp.float32)
    base = jnp.clip(base, -4.0, 4.0)
    channel_scale = jnp.exp(jax.random.uniform(key_scale, (1, CH, 1), jnp.float32, 0.0, math.log(10.0)))
    envelope = jnp.exp(jax.random.uniform(key_env, (W, CH, 16), jnp.float32, 0.0, math.log(10.0)))
    envelope = jnp.repeat(envelope, L // 16, axis=2)
    return (base * channel_scale * envelope).astype(jnp.bfloat16)


def draw_channel_of_row(key, part):
    groups = CH // CHB
    keys = jax.random.split(key, groups)
    perms = jax.vmap(lambda one_key: jax.random.permutation(one_key, CHB))(keys).astype(jnp.int32)
    offsets = jnp.arange(groups, dtype=jnp.int32)[:, None]
    return (offsets + groups * perms).reshape(CH)


def set_ends(drawn, own_key, smallest, top_value):
    longest = drawn.shape.index(max(drawn.shape))
    spots = []
    for shift in (0, 1):
        where = [jax.random.randint(jax.random.fold_in(own_key, axis), (), 0, length) for axis, length in enumerate(drawn.shape)]
        where[longest] = (where[longest] + shift) % drawn.shape[longest]
        spots.append(tuple(where))
    return drawn.at[spots[0]].set(smallest).at[spots[1]].set(top_value)


def setup_inputs(seed: int = 0) -> dict:
    key_list = jax.random.split(jax.random.key(seed), 6)
    raw_samples = draw_raw_samples(jax.random.fold_in(key_list[5], 71), 0)
    channel_of_row = draw_channel_of_row(jax.random.fold_in(key_list[5], 71), 0)
    live_channels = set_ends((jax.random.randint(key_list[2], (CH,), 0, 8) < 7).astype(jnp.int32), jax.random.fold_in(key_list[2], 1), 0, 1)
    band_reach = set_ends(jax.random.randint(key_list[3], (CH,), 1, BAND), jax.random.fold_in(key_list[3], 1), 1, BAND - 1).astype(jnp.int32)
    bin_taper = jnp.clip(jnp.exp(jax.random.uniform(key_list[4], (F,), jnp.float32, math.log(0.5), math.log(2.0))), 0.5, 2.0)
    return {"raw_samples": raw_samples, "channel_of_row": channel_of_row, "live_channels": live_channels, "band_reach": band_reach, "bin_taper": bin_taper}


norm_floor = 1e-05
water_level = 0.3

def basis_table():
    sample_index = jnp.arange(L, dtype=jnp.int32)
    bin_index = jnp.arange(F, dtype=jnp.int32) + K0
    phase = jnp.mod(sample_index[:, None] * bin_index[None, :], L)
    angle = phase.astype(jnp.float32) * (2.0 * math.pi / L)
    return jnp.concatenate([jnp.cos(angle), -jnp.sin(angle)], axis=1).astype(jnp.bfloat16)

def lag_table():
    bin_index = jnp.arange(F, dtype=jnp.int32) + K0
    lag_index = jnp.arange(LAGS, dtype=jnp.int32) - LAGS // 2
    phase = jnp.mod(bin_index[:, None] * lag_index[None, :], L)
    angle = phase.astype(jnp.float32) * (2.0 * math.pi / L)
    table = jnp.concatenate([jnp.cos(angle), jnp.sin(angle)], axis=0) * (1.0 / math.sqrt(F))
    return table.astype(jnp.bfloat16)

def whiten_window(samples, bin_taper):
    values = samples.astype(jnp.float32)
    magnitude = jnp.abs(values)
    running = jnp.cumsum(magnitude, axis=1)
    running = jnp.concatenate([jnp.zeros((samples.shape[0], 1), jnp.float32), running], axis=1)
    positions = jnp.arange(L, dtype=jnp.int32)
    upper = jnp.minimum(positions + HW, L - 1)
    lower = jnp.maximum(positions - HW, 0)
    window_sum = running[:, upper + 1] - running[:, lower]
    counts = (upper - lower + 1).astype(jnp.float32)
    normed = (values / (window_sum / counts + norm_floor)).astype(jnp.bfloat16)
    spectrum = jnp.dot(normed, basis_table(), preferred_element_type=jnp.float32)
    real_part = spectrum[:, :F]
    imag_part = spectrum[:, F:]
    amplitude = jnp.sqrt(real_part * real_part + imag_part * imag_part)
    padded = jnp.pad(amplitude, ((0, 0), (1, 1)))
    neighbours = padded[:, :-2] + padded[:, 1:-1] + padded[:, 2:]
    bins = jnp.arange(F, dtype=jnp.int32)
    bin_counts = jnp.where((bins == 0) | (bins == F - 1), 2.0, 3.0).astype(jnp.float32)
    smooth = neighbours / bin_counts
    level = jnp.maximum(smooth, water_level * (lax.optimization_barrier(jnp.mean(amplitude, axis=1, keepdims=True)) + norm_floor))
    factor = bin_taper[None, :] / level
    return jnp.concatenate([real_part * factor, imag_part * factor], axis=1).astype(jnp.bfloat16)

def reference(raw_samples, channel_of_row, live_channels, band_reach, bin_taper):
    acquired = lax.map(lambda samples: whiten_window(samples, bin_taper), raw_samples)
    inverse = jnp.argsort(channel_of_row).astype(jnp.int32)
    white = jnp.take(acquired, inverse, axis=1)
    white = white * live_channels.astype(jnp.bfloat16)[None, :, None]
    padded = jnp.concatenate([white, jnp.zeros((W, N_RCV * CHB, 2 * F), jnp.bfloat16)], axis=1)
    lag_basis = lag_table().astype(jnp.float32)
    scale = 1.0 / math.sqrt(W)

    def one_block(block_index):
        start = (block_index * CHB).astype(jnp.int32)
        sources = lax.dynamic_slice_in_dim(white, start, CHB, 1).astype(jnp.float32)
        receivers = lax.dynamic_slice_in_dim(padded, start, N_RCV * CHB, 1).astype(jnp.float32)
        src_real = sources[..., :F]
        src_imag = sources[..., F:]
        left = jnp.concatenate([src_real, src_imag], axis=0)
        left_imag = jnp.concatenate([src_imag, -src_real], axis=0)
        right = jnp.concatenate([receivers[..., :F], receivers[..., F:]], axis=0)
        cross_real = jnp.einsum('kif,kjf->ijf', left, right, precision=lax.Precision.HIGHEST)
        cross_imag = jnp.einsum('kif,kjf->ijf', left_imag, right, precision=lax.Precision.HIGHEST)
        stacked = (jnp.concatenate([cross_real, cross_imag], axis=2) * scale).astype(jnp.bfloat16)
        lagged = jnp.einsum('ijg,gc->ijc', stacked.astype(jnp.float32), lag_basis, precision=lax.Precision.HIGHEST)
        source_index = start + jnp.arange(CHB, dtype=jnp.int32)
        receiver_index = start + jnp.arange(N_RCV * CHB, dtype=jnp.int32)
        gap = receiver_index[None, :] - source_index[:, None]
        reach_rows = lax.dynamic_slice_in_dim(band_reach, start, CHB)
        keep = (gap >= 0) & (gap <= reach_rows[:, None])
        result = jnp.where(keep[:, :, None], lagged, 0.0).astype(jnp.bfloat16)
        return result.reshape(CHB, N_RCV * CHB * LAGS)
    blocks = lax.map(one_block, jnp.arange(N_SRC, dtype=jnp.int32))
    return blocks.reshape(CH, N_RCV * CHB * LAGS)
```

```python
import functools
import math

import jax
import jax.numpy as jnp
import ml_dtypes
import numpy as np
from jax import lax
from jax.experimental import pallas as pl
from jax.experimental.pallas import tpu as pltpu
from jax.sharding import PartitionSpec as P

F = 64
K0 = 32
HW = 64
LAGS = 32
CHUNK = 16

norm_floor = 1e-05
water_level = 0.3


def basis_table(length):
    sample_index = np.arange(length)
    bin_index = np.arange(F) + K0
    phase = np.mod(sample_index[:, None] * bin_index[None, :], length)
    angle = phase * (2.0 * math.pi / length)
    table = np.concatenate([np.cos(angle), -np.sin(angle)], axis=1)
    return table.astype(np.float32).astype(ml_dtypes.bfloat16)


def lag_tables(length):
    bin_index = np.arange(F) + K0
    lag_index = np.arange(LAGS) - LAGS // 2
    phase = np.mod(lag_index[:, None] * bin_index[None, :], length)
    angle = phase * (2.0 * math.pi / length)
    scale = 1.0 / math.sqrt(F)
    cosine = (np.cos(angle) * scale).astype(np.float32).astype(ml_dtypes.bfloat16)
    sine = (np.sin(angle) * scale).astype(np.float32).astype(ml_dtypes.bfloat16)
    straight = np.concatenate([cosine, cosine], axis=1).astype(np.float32)
    swapped = np.concatenate([-sine, sine], axis=1).astype(np.float32)
    return straight, swapped


def inverse_counts(length):
    positions = np.arange(length)
    upper = np.minimum(positions + HW, length - 1)
    lower = np.maximum(positions - HW, 0)
    return (1.0 / (upper - lower + 1)).astype(np.float32)[None, :]


def band(rows, columns, shift):
    row = lax.broadcasted_iota(jnp.int32, (rows, columns), 0)
    column = lax.broadcasted_iota(jnp.int32, (rows, columns), 1)
    return (jnp.abs(row - column - shift) <= HW).astype(jnp.float32).astype(jnp.bfloat16)


def whiten_kernel(src_count, x_ref, channel_ref, taper_ref, inverse_ref, basis_ref, out_ref, normed_ref):
    samples = x_ref[0]
    rows, length = samples.shape
    width = 256
    for start in range(0, length, width):
        low = max(start - 128, 0)
        high = min(start + width + 128, length)
        magnitude = jnp.abs(x_ref[0, :, low:high])
        total = jnp.dot(
            magnitude, band(high - low, width, start - low), preferred_element_type=jnp.float32
        )
        level = total * inverse_ref[:, start : start + width] + norm_floor
        values = x_ref[0, :, start : start + width].astype(jnp.float32)
        normed_ref[:, start : start + width] = (values / level).astype(jnp.bfloat16)
    spectrum = jnp.dot(normed_ref[...], basis_ref[...], preferred_element_type=jnp.float32)
    square = spectrum * spectrum
    amplitude = jnp.sqrt(square + pltpu.roll(square, F, 1))
    bins = lax.broadcasted_iota(jnp.int32, (1, 2 * F), 1) % F
    first, last = bins == 0, bins == F - 1
    below = jnp.where(first, 0.0, pltpu.roll(amplitude, 1, 1))
    above = jnp.where(last, 0.0, pltpu.roll(amplitude, 2 * F - 1, 1))
    share = jnp.where(first | last, 1.0 / 2.0, 1.0 / 3.0)
    smooth = (below + amplitude + above) * share
    mean = jnp.sum(amplitude, axis=1, keepdims=True) * (0.5 / F)
    level = jnp.maximum(smooth, water_level * (mean + norm_floor))
    white = (spectrum * (taper_ref[...] / level)).astype(jnp.bfloat16)
    floor = lax.broadcasted_iota(jnp.int32, (rows, rows), 0) * src_count
    channel = channel_ref[...]
    pick = (channel >= floor) & (channel < floor + src_count)
    pick = pick.astype(jnp.float32).astype(jnp.bfloat16)
    ordered = jnp.dot(pick, white, preferred_element_type=jnp.float32).astype(jnp.bfloat16)
    out_ref[:, 0] = ordered.reshape(src_count, rows // src_count, 2 * F)


def whiten(raw_samples, channel_of_row, bin_taper, src_count):
    windows, rows, length = raw_samples.shape
    part = rows // src_count
    whole = lambda *shape: pl.BlockSpec(shape, lambda w: (0,) * len(shape))
    return pl.pallas_call(
        functools.partial(whiten_kernel, src_count),
        grid=(windows,),
        out_shape=jax.ShapeDtypeStruct((src_count, windows, part, 2 * F), jnp.bfloat16),
        in_specs=[
            pl.BlockSpec((1, rows, length), lambda w: (w, 0, 0)),
            whole(1, rows),
            whole(1, 2 * F),
            whole(1, length),
            whole(length, 2 * F),
        ],
        out_specs=pl.BlockSpec((src_count, 1, part, 2 * F), lambda w: (0, w, 0, 0)),
        scratch_shapes=[pltpu.VMEM((rows, length), jnp.bfloat16)],
        compiler_params=pltpu.CompilerParams(vmem_limit_bytes=40 << 20),
        name="whiten",
    )(
        raw_samples,
        channel_of_row.reshape(1, rows),
        jnp.tile(bin_taper, 2).reshape(1, 2 * F),
        jnp.asarray(inverse_counts(length)),
        jnp.asarray(basis_table(length)),
    )


def correlate_kernel(pieces, windows, scale, *refs):
    src_refs, rcv_refs = refs[:pieces], refs[pieces : 2 * pieces]
    reach_ref, straight_ref, swapped_ref, out_ref = refs[2 * pieces : 2 * pieces + 4]
    left_ref, rcv_ref, turned_ref, even_ref, odd_ref = refs[2 * pieces + 4 :]
    step = pl.program_id(0)
    src_count, local, part, lanes = src_refs[0].shape
    rows = src_count * part
    columns = CHUNK * LAGS

    def rotate(first, target):
        straight = straight_ref[...][None]
        swapped = swapped_ref[...][None]
        for w in range(windows):
            plain = rcv_ref[w, pl.ds(first, CHUNK), :]
            turned = turned_ref[w, pl.ds(first, CHUNK), :]
            value = plain[:, None, :] * straight + turned[:, None, :] * swapped
            target[:, w * lanes : (w + 1) * lanes] = value.reshape(columns, lanes).astype(
                jnp.bfloat16
            )

    @pl.when(step == 0)
    def _():
        natural = lax.broadcasted_iota(jnp.int32, (rows, rows), 0)
        held = lax.broadcasted_iota(jnp.int32, (rows, rows), 1)
        pick = natural == (held % part) * src_count + held // part
        pick = pick.astype(jnp.float32).astype(jnp.bfloat16)
        for d in range(pieces):
            for n in range(local):
                w = d * local + n
                block = src_refs[d][:, n].reshape(rows, lanes)
                left_ref[:, w * lanes : (w + 1) * lanes] = jnp.dot(
                    pick, block, preferred_element_type=jnp.float32
                ).astype(jnp.bfloat16)
                block = rcv_refs[d][:, n].reshape(rows, lanes)
                value = jnp.dot(pick, block, preferred_element_type=jnp.float32)
                rcv_ref[w] = value
                turned_ref[w] = pltpu.roll(value, F, 1)
        rotate(0, even_ref)

    shift = lax.axis_index("rcv") * rows
    low = (lax.broadcasted_iota(jnp.int32, (rows, 1), 0) - shift) * LAGS
    high = low + reach_ref[...] * LAGS + (LAGS - 1)

    def multiply(source, half):
        total = lax.dot_general(
            left_ref[...], source[...], (((1,), (1,)), ((), ())), preferred_element_type=jnp.float32
        )
        column = lax.broadcasted_iota(jnp.int32, (1, columns), 1)
        column = column + (2 * step + half) * columns
        keep = (column >= low) & (column <= high)
        out_ref[:, half * columns : (half + 1) * columns] = jnp.where(
            keep, total * scale, 0.0
        ).astype(jnp.bfloat16)

    multiply(even_ref, 0)
    rotate((2 * step + 1) * CHUNK, odd_ref)
    multiply(odd_ref, 1)
    rotate(jnp.minimum(2 * step + 2, rows // CHUNK - 1) * CHUNK, even_ref)


def correlate(src_pieces, rcv_pieces, band_reach, length):
    pieces = len(src_pieces)
    src_count, local, part, lanes = src_pieces[0].shape
    rows = src_count * part
    windows = pieces * local
    straight, swapped = lag_tables(length)
    whole = lambda *shape: pl.BlockSpec(shape, lambda g: (0,) * len(shape))
    columns = CHUNK * LAGS
    depth = windows * lanes
    return pl.pallas_call(
        functools.partial(correlate_kernel, pieces, windows, 1.0 / math.sqrt(windows)),
        grid=(rows // (2 * CHUNK),),
        out_shape=jax.ShapeDtypeStruct((rows, rows * LAGS), jnp.bfloat16),
        in_specs=[whole(src_count, local, part, lanes)] * (2 * pieces)
        + [whole(rows, 1), whole(LAGS, lanes), whole(LAGS, lanes)],
        out_specs=pl.BlockSpec((rows, 2 * columns), lambda g: (0, g)),
        scratch_shapes=[
            pltpu.VMEM((rows, depth), jnp.bfloat16),
            pltpu.VMEM((windows, rows, lanes), jnp.float32),
            pltpu.VMEM((windows, rows, lanes), jnp.float32),
            pltpu.VMEM((columns, depth), jnp.bfloat16),
            pltpu.VMEM((columns, depth), jnp.bfloat16),
        ],
        compiler_params=pltpu.CompilerParams(vmem_limit_bytes=56 << 20),
        name="correlate",
    )(
        *src_pieces,
        *rcv_pieces,
        band_reach.reshape(rows, 1),
        jnp.asarray(straight),
        jnp.asarray(swapped),
    )


def body(raw_samples, channel_of_row, live_channels, band_reach, bin_taper):
    src_count = lax.axis_size("src")
    rcv_count = lax.axis_size("rcv")
    windows, rows, length = raw_samples.shape
    part = rows // src_count
    ordered = whiten(raw_samples, channel_of_row, bin_taper, src_count)
    arrived = lax.all_to_all(ordered, "src", split_axis=0, concat_axis=0, tiled=True)
    live = live_channels.reshape(part, src_count).T.astype(jnp.bfloat16)
    own = arrived * live[:, None, :, None]
    src_pieces, rcv_pieces = [own], []
    for d in range(rcv_count):
        if d:
            route = [(i, (i + d) % rcv_count) for i in range(rcv_count)]
            src_pieces.append(lax.ppermute(own, "rcv", route))
        route = []
        for s in range(src_count):
            for r in range(rcv_count):
                to = (r + d) % rcv_count
                if s >= to:
                    route.append((s * rcv_count + r, (s - to) * rcv_count + to))
        rcv_pieces.append(lax.ppermute(own, ("src", "rcv"), route))
    return correlate(src_pieces, rcv_pieces, band_reach, length)


def solution(mesh):
    return jax.shard_map(
        body,
        mesh=mesh,
        in_specs=(P("rcv", "src", None), P("src"), P("src"), P("src"), P()),
        out_specs=P("src", "rcv"),
        check_vma=False,
    )
```

```python
import functools
import math

import jax
import jax.numpy as jnp
import ml_dtypes
import numpy as np
from jax import lax
from jax.experimental import pallas as pl
from jax.experimental.pallas import tpu as pltpu
from jax.sharding import PartitionSpec as P

F = 64
K0 = 32
HW = 64
LAGS = 32
CHUNK = 16

norm_floor = 1e-05
water_level = 0.3


def basis_table(length):
    sample_index = np.arange(length)
    bin_index = np.arange(F) + K0
    phase = np.mod(sample_index[:, None] * bin_index[None, :], length)
    angle = phase * (2.0 * math.pi / length)
    table = np.concatenate([np.cos(angle), -np.sin(angle)], axis=1)
    return table.astype(np.float32).astype(ml_dtypes.bfloat16)


def lag_tables(length):
    bin_index = np.arange(F) + K0
    lag_index = np.arange(LAGS) - LAGS // 2
    phase = np.mod(lag_index[:, None] * bin_index[None, :], length)
    angle = phase * (2.0 * math.pi / length)
    scale = 1.0 / math.sqrt(F)
    cosine = (np.cos(angle) * scale).astype(np.float32).astype(ml_dtypes.bfloat16)
    sine = (np.sin(angle) * scale).astype(np.float32).astype(ml_dtypes.bfloat16)
    straight = np.concatenate([cosine, cosine], axis=1).astype(np.float32)
    swapped = np.concatenate([-sine, sine], axis=1).astype(np.float32)
    return straight, swapped


def inverse_counts(length):
    positions = np.arange(length)
    upper = np.minimum(positions + HW, length - 1)
    lower = np.maximum(positions - HW, 0)
    return (1.0 / (upper - lower + 1)).astype(np.float32)[None, :]


def band(rows, columns, shift):
    row = lax.broadcasted_iota(jnp.int32, (rows, columns), 0)
    column = lax.broadcasted_iota(jnp.int32, (rows, columns), 1)
    return (jnp.abs(row - column - shift) <= HW).astype(jnp.float32).astype(jnp.bfloat16)


def whiten_window(w, src_count, x_ref, channel_ref, taper_ref, inverse_ref, basis_ref, normed_ref):
    rows, length = x_ref.shape[1:]
    width = 256
    for start in range(0, length, width):
        low = max(start - 128, 0)
        high = min(start + width + 128, length)
        magnitude = jnp.abs(x_ref[w, :, low:high])
        total = jnp.dot(
            magnitude, band(high - low, width, start - low), preferred_element_type=jnp.float32
        )
        level = total * inverse_ref[:, start : start + width] + norm_floor
        values = x_ref[w, :, start : start + width].astype(jnp.float32)
        normed_ref[:, start : start + width] = (values / level).astype(jnp.bfloat16)
    spectrum = jnp.dot(normed_ref[...], basis_ref[...], preferred_element_type=jnp.float32)
    square = spectrum * spectrum
    amplitude = jnp.sqrt(square + pltpu.roll(square, F, 1))
    bins = lax.broadcasted_iota(jnp.int32, (1, 2 * F), 1) % F
    first, last = bins == 0, bins == F - 1
    below = jnp.where(first, 0.0, pltpu.roll(amplitude, 1, 1))
    above = jnp.where(last, 0.0, pltpu.roll(amplitude, 2 * F - 1, 1))
    share = jnp.where(first | last, 1.0 / 2.0, 1.0 / 3.0)
    smooth = (below + amplitude + above) * share
    mean = jnp.sum(amplitude, axis=1, keepdims=True) * (0.5 / F)
    level = jnp.maximum(smooth, water_level * (mean + norm_floor))
    white = (spectrum * (taper_ref[...] / level)).astype(jnp.bfloat16)
    floor = lax.broadcasted_iota(jnp.int32, (rows, rows), 0) * src_count
    channel = channel_ref[...]
    pick = (channel >= floor) & (channel < floor + src_count)
    pick = pick.astype(jnp.float32).astype(jnp.bfloat16)
    ordered = jnp.dot(pick, white, preferred_element_type=jnp.float32).astype(jnp.bfloat16)
    return ordered.reshape(src_count, rows // src_count, 2 * F)


def spread_kernel(
    src_count, rcv_count, x_ref, channel_ref, taper_ref, inverse_ref, basis_ref, live_ref,
    block_ref, near_ref, rest_ref,
    normed_ref, ordered_ref, arrived_ref, own_ref,
    swap_send, swap_recv, block_send, block_recv, pass_send, near_send, near_recv, local_sem,
):
    src, rcv = lax.axis_index("src"), lax.axis_index("rcv")
    windows = x_ref.shape[0]
    half = own_ref.shape[3]
    pairs = rcv_count // 2
    row, core = rcv // 2, rcv % 2
    mate = rcv + 1 - 2 * core

    def slot(receiver, holder):
        return (receiver + rcv_count - holder) % rcv_count

    def signal(place):
        pl.semaphore_signal(barrier, inc=1, device_id=place, device_id_type=pl.DeviceIdType.MESH)

    def push(source, target, send_sem, recv_sem, place):
        return pltpu.make_async_remote_copy(
            src_ref=source,
            dst_ref=target,
            send_sem=send_sem,
            recv_sem=recv_sem,
            device_id=place,
            device_id_type=pl.DeviceIdType.MESH,
        )

    barrier = pltpu.get_barrier_semaphore()
    for k in range(1, src_count):
        signal(((src + k) % src_count, rcv))
    for k in range(1, rcv_count):
        signal((src, (rcv + k) % rcv_count))
    takes = (rcv >= 1) & (src + rcv < src_count)

    @pl.when(takes)
    def _():
        for k in range(rcv_count):
            signal((src + rcv, k))

    pl.semaphore_wait(
        barrier, src_count - 1 + rcv_count - 1 + jnp.minimum(src, rcv_count - 1)
    )

    def swap(w, k):
        target = (src + k) % src_count
        return push(
            ordered_ref.at[w, target],
            arrived_ref.at[w, src],
            swap_send.at[w, k],
            swap_recv.at[w, src],
            (target, rcv),
        )

    def swapped(w, k):
        source = (src + k) % src_count
        return push(
            ordered_ref.at[w, source],
            arrived_ref.at[w, source],
            swap_send.at[w, k],
            swap_recv.at[w, source],
            (source, rcv),
        )

    def share(w, k):
        to = mate if k == 0 else ((row + k) % pairs) * 2 + core
        place = slot(to, rcv)
        return push(
            own_ref.at[w], block_ref.at[place, w], block_send.at[w, k], block_recv.at[w, place], (src, to)
        )

    def shared(w, holder):
        place = slot(rcv, holder)
        return push(
            own_ref.at[w], block_ref.at[place, w], block_send.at[w, 0], block_recv.at[w, place], (src, mate)
        )

    def hand_on(w, k):
        holder = ((row + k) % pairs) * 2 + core
        place = slot(mate, holder)
        return push(
            block_ref.at[slot(rcv, holder), w],
            block_ref.at[place, w],
            pass_send.at[w, k],
            block_recv.at[w, place],
            (src, mate),
        )

    def near(w, to):
        place = slot(to, rcv)
        return push(
            own_ref.at[w, 0],
            near_ref.at[place, w],
            near_send.at[w, to],
            near_recv.at[w, place],
            (src - to, to),
        )

    def keep(w):
        return pltpu.make_async_copy(own_ref.at[w], block_ref.at[0, w], local_sem.at[w])

    for w in range(windows):
        ordered_ref[w] = whiten_window(
            w, src_count, x_ref, channel_ref, taper_ref, inverse_ref, basis_ref, normed_ref
        )
        for k in range(1, src_count):
            swap(w, k).start()

    for w in range(windows):
        for k in range(src_count):
            source = (src + k) % src_count
            if k:
                swapped(w, k).wait_recv()
                value = arrived_ref[w, source]
            else:
                value = ordered_ref[w, source]
            value = value * live_ref[source]
            own_ref[w, 0, source] = value[:half]
            own_ref[w, 1, source] = value[half:]
            rest_ref[w, source] = value[half:]
        for k in range(pairs):
            share(w, (k + 1) % pairs).start()
        for to in range(1, rcv_count):
            pl.when(src >= to)(lambda w=w, to=to: near(w, to).start())
        keep(w).start()

    for w in range(windows):
        for k in range(1, pairs):
            shared(w, ((row + k) % pairs) * 2 + core).wait_recv()
            hand_on(w, k).start()

    for w in range(windows):
        for k in range(pairs):
            shared(w, ((row + k) % pairs) * 2 + 1 - core).wait_recv()

        @pl.when(takes)
        def _(w=w):
            for k in range(rcv_count):
                push(
                    own_ref.at[w, 0], near_ref.at[k, w], near_send.at[w, 0], near_recv.at[w, k], (src + rcv, k)
                ).wait_recv()

        for k in range(1, src_count):
            swap(w, k).wait_send()
        for k in range(pairs):
            share(w, k).wait_send()
            if k:
                hand_on(w, k).wait_send()
        for to in range(1, rcv_count):
            pl.when(src >= to)(lambda w=w, to=to: near(w, to).wait_send())
        keep(w).wait()


def spread(raw_samples, channel_of_row, live_channels, bin_taper, src_count, rcv_count):
    windows, rows, length = raw_samples.shape
    part = rows // src_count
    half = part // 2
    lanes = 2 * F
    live = live_channels.reshape(part, src_count).T.astype(jnp.bfloat16)
    live = jnp.broadcast_to(live[:, None, :, None], (src_count, 1, part, lanes)).reshape(
        src_count, part, lanes
    )
    vmem = pl.BlockSpec(memory_space=pltpu.VMEM)
    anywhere = pl.BlockSpec(memory_space=pl.ANY)
    dma = pltpu.SemaphoreType.DMA
    return pl.pallas_call(
        functools.partial(spread_kernel, src_count, rcv_count),
        out_shape=[
            jax.ShapeDtypeStruct((rcv_count, windows, 2, src_count, half, lanes), jnp.bfloat16),
            jax.ShapeDtypeStruct((rcv_count, windows, src_count, half, lanes), jnp.bfloat16),
            jax.ShapeDtypeStruct((windows, src_count, half, lanes), jnp.bfloat16),
        ],
        in_specs=[vmem] * 6,
        out_specs=[anywhere, anywhere, vmem],
        scratch_shapes=[
            pltpu.VMEM((rows, length), jnp.bfloat16),
            pltpu.VMEM((windows, src_count, part, lanes), jnp.bfloat16),
            pltpu.VMEM((windows, src_count, part, lanes), jnp.bfloat16),
            pltpu.VMEM((windows, 2, src_count, half, lanes), jnp.bfloat16),
            dma((windows, src_count)),
            dma((windows, src_count)),
            dma((windows, rcv_count // 2)),
            dma((windows, rcv_count)),
            dma((windows, rcv_count // 2)),
            dma((windows, rcv_count)),
            dma((windows, rcv_count)),
            dma((windows,)),
        ],
        compiler_params=pltpu.CompilerParams(
            collective_id=0, has_side_effects=True, vmem_limit_bytes=48 << 20
        ),
        name="spread",
    )(
        raw_samples,
        channel_of_row.reshape(1, rows),
        jnp.tile(bin_taper, 2).reshape(1, lanes),
        jnp.asarray(inverse_counts(length)),
        jnp.asarray(basis_table(length)),
        live,
    )


def correlate_kernel(pieces, half_index, scale, *refs):
    refs = list(refs)
    block_ref = refs.pop(0)
    rcv_refs = [refs.pop(0) for _ in range(pieces if half_index else 1)]
    reach_ref, straight_ref, swapped_ref = refs[:3]
    if half_index:
        left_ref, _, out_ref = refs[3:6]
    else:
        out_ref, left_ref = refs[3:5]
    rcv_ref, turned_ref, even_ref, odd_ref = refs[-4:]
    step = pl.program_id(0)
    local, halves, src_count, half, lanes = block_ref.shape[1:]
    windows = pieces * local
    count = src_count * half
    rows = halves * count
    columns = CHUNK * LAGS
    src, rcv = lax.axis_index("src"), lax.axis_index("rcv")

    def rotate(first, target):
        straight = straight_ref[...][None]
        swapped = swapped_ref[...][None]
        for w in range(windows):
            plain = rcv_ref[pl.ds(first, CHUNK), w * lanes : (w + 1) * lanes]
            turned = turned_ref[pl.ds(first, CHUNK), w * lanes : (w + 1) * lanes]
            value = plain[:, None, :] * straight + turned[:, None, :] * swapped
            target[:, w * lanes : (w + 1) * lanes] = value.reshape(columns, lanes).astype(
                jnp.bfloat16
            )

    @pl.when(step == 0)
    def _():
        natural = lax.broadcasted_iota(jnp.int32, (count, count), 0)
        held = lax.broadcasted_iota(jnp.int32, (count, count), 1)
        pick = natural == (held % half) * src_count + held // half
        pick = pick.astype(jnp.float32).astype(jnp.bfloat16)
        for d in range(pieces):
            span = slice(d * local * lanes, (d + 1) * local * lanes)
            own = [
                jnp.concatenate(
                    [block_ref[d, n, h].reshape(count, lanes) for n in range(local)], axis=1
                )
                for h in range(halves)
            ]
            if not half_index:
                for h in range(halves):
                    left_ref[h * count : (h + 1) * count, span] = jnp.dot(
                        pick, own[h], preferred_element_type=jnp.float32
                    ).astype(jnp.bfloat16)
            source = rcv_refs[d] if half_index else rcv_refs[0].at[d]
            other = jnp.concatenate(
                [source[n].reshape(count, lanes) for n in range(local)], axis=1
            )
            block = jnp.where(rcv == 0, own[half_index], other)
            value = jnp.dot(pick, block, preferred_element_type=jnp.float32)
            rcv_ref[:, span] = value
            for n in range(local):
                at = (d * local + n) * lanes
                turned_ref[:, at : at + lanes] = pltpu.roll(
                    value[:, n * lanes : (n + 1) * lanes], F, 1
                )
        rotate(0, even_ref)

    low = (lax.broadcasted_iota(jnp.int32, (rows, 1), 0) - rcv * rows) * LAGS
    high = low + reach_ref[...] * LAGS + (LAGS - 1)
    high = jnp.where(src + rcv < src_count, high, -1)

    def multiply(source, turn):
        total = lax.dot_general(
            left_ref[...], source[...], (((1,), (1,)), ((), ())), preferred_element_type=jnp.float32
        )
        column = lax.broadcasted_iota(jnp.int32, (1, columns), 1)
        column = column + (2 * step + turn) * columns + half_index * count * LAGS
        keep = (column >= low) & (column <= high)
        out_ref[:, turn * columns : (turn + 1) * columns] = jnp.where(
            keep, total * scale, 0.0
        ).astype(jnp.bfloat16)

    multiply(even_ref, 0)
    rotate((2 * step + 1) * CHUNK, odd_ref)
    multiply(odd_ref, 1)
    rotate(jnp.minimum(2 * step + 2, count // CHUNK - 1) * CHUNK, even_ref)


def correlate(block, receivers, band_reach, length, earlier=None):
    half_index = int(earlier is not None)
    pieces, local, halves, src_count, half, lanes = block.shape
    count = src_count * half
    rows = halves * count
    windows = pieces * local
    depth = windows * lanes
    columns = CHUNK * LAGS
    steps = count // (2 * CHUNK)
    straight, swapped = lag_tables(length)
    whole = lambda *shape: pl.BlockSpec(shape, lambda g: (0,) * len(shape))
    operands = [
        block, *receivers, band_reach.reshape(rows, 1), jnp.asarray(straight), jnp.asarray(swapped)
    ]
    in_specs = [whole(*operand.shape) for operand in operands]
    out_shape = [jax.ShapeDtypeStruct((rows, rows * LAGS), jnp.bfloat16)]
    out_specs = [pl.BlockSpec((rows, 2 * columns), lambda g: (0, g + half_index * steps))]
    aliases = {}
    if half_index:
        operands += [earlier[1], earlier[0]]
        in_specs += [whole(rows, depth), pl.BlockSpec(memory_space=pl.ANY)]
        aliases = {len(operands) - 1: 0}
    else:
        out_shape.append(jax.ShapeDtypeStruct((rows, depth), jnp.bfloat16))
        out_specs.append(whole(rows, depth))
    return pl.pallas_call(
        functools.partial(correlate_kernel, pieces, half_index, 1.0 / math.sqrt(windows)),
        grid=(steps,),
        out_shape=out_shape,
        in_specs=in_specs,
        out_specs=out_specs,
        scratch_shapes=[
            pltpu.VMEM((count, depth), jnp.float32),
            pltpu.VMEM((count, depth), jnp.float32),
            pltpu.VMEM((columns, depth), jnp.bfloat16),
            pltpu.VMEM((columns, depth), jnp.bfloat16),
        ],
        input_output_aliases=aliases,
        cost_estimate=pl.CostEstimate(
            flops=2 * rows * depth * count * LAGS,
            bytes_accessed=2 * rows * count * LAGS,
            transcendentals=0,
        ),
        compiler_params=pltpu.CompilerParams(vmem_limit_bytes=56 << 20),
        name="correlate",
    )(*operands)


def body(raw_samples, channel_of_row, live_channels, band_reach, bin_taper):
    src_count = lax.axis_size("src")
    rcv_count = lax.axis_size("rcv")
    length = raw_samples.shape[2]
    block, near, rest = spread(
        raw_samples, channel_of_row, live_channels, bin_taper, src_count, rcv_count
    )
    far = []
    for d in range(rcv_count):
        route = []
        for s in range(src_count):
            for r in range(rcv_count):
                to = (r + d) % rcv_count
                if to and s >= to:
                    route.append((s * rcv_count + r, (s - to) * rcv_count + to))
        far.append(lax.ppermute(rest, ("src", "rcv"), route))
    earlier = correlate(block, [near], band_reach, length)
    return correlate(block, far, band_reach, length, earlier)[0]


def solution(mesh):
    return jax.shard_map(
        body,
        mesh=mesh,
        in_specs=(P("rcv", "src", None), P("src"), P("src"), P("src"), P()),
        out_specs=P("src", "rcv"),
        check_vma=False,
    )
```

```python
import functools
import math

import jax
import jax.numpy as jnp
import ml_dtypes
import numpy as np
from jax import lax
from jax.experimental import pallas as pl
from jax.experimental.pallas import tpu as pltpu
from jax.sharding import PartitionSpec as P

F = 64
K0 = 32
HW = 64
LAGS = 32
CHUNK = 16

norm_floor = 1e-05
water_level = 0.3


def basis_table(length):
    sample_index = np.arange(length)
    bin_index = np.arange(F) + K0
    phase = np.mod(sample_index[:, None] * bin_index[None, :], length)
    angle = phase * (2.0 * math.pi / length)
    table = np.concatenate([np.cos(angle), -np.sin(angle)], axis=1)
    return table.astype(np.float32).astype(ml_dtypes.bfloat16)


def lag_tables(length):
    bin_index = np.arange(F) + K0
    lag_index = np.arange(LAGS) - LAGS // 2
    phase = np.mod(lag_index[:, None] * bin_index[None, :], length)
    angle = phase * (2.0 * math.pi / length)
    scale = 1.0 / math.sqrt(F)
    cosine = (np.cos(angle) * scale).astype(np.float32).astype(ml_dtypes.bfloat16)
    sine = (np.sin(angle) * scale).astype(np.float32).astype(ml_dtypes.bfloat16)
    straight = np.concatenate([cosine, cosine], axis=1).astype(np.float32)
    swapped = np.concatenate([-sine, sine], axis=1).astype(np.float32)
    return straight, swapped


def inverse_counts(start, width, length):
    position = lax.broadcasted_iota(jnp.int32, (1, width), 1) + start
    upper = jnp.minimum(position + HW, length - 1)
    lower = jnp.maximum(position - HW, 0)
    return 1.0 / (upper - lower + 1).astype(jnp.float32)


def band(rows, columns, shift):
    row = lax.broadcasted_iota(jnp.int32, (rows, columns), 0)
    column = lax.broadcasted_iota(jnp.int32, (rows, columns), 1)
    return (jnp.abs(row - column - shift) <= HW).astype(jnp.float32).astype(jnp.bfloat16)


def whiten_window(w, src_count, x_ref, channel_ref, taper_ref, basis_ref, normed_ref):
    rows, length = x_ref.shape[1:]
    width = 256
    for start in range(0, length, width):
        low = max(start - 128, 0)
        high = min(start + width + 128, length)
        magnitude = jnp.abs(x_ref[w, :, low:high])
        total = jnp.dot(
            magnitude, band(high - low, width, start - low), preferred_element_type=jnp.float32
        )
        level = total * inverse_counts(start, width, length) + norm_floor
        values = x_ref[w, :, start : start + width].astype(jnp.float32)
        normed_ref[:, start : start + width] = (values / level).astype(jnp.bfloat16)
    spectrum = jnp.dot(normed_ref[...], basis_ref[...], preferred_element_type=jnp.float32)
    square = spectrum * spectrum
    amplitude = jnp.sqrt(square + pltpu.roll(square, F, 1))
    bins = lax.broadcasted_iota(jnp.int32, (1, 2 * F), 1) % F
    first, last = bins == 0, bins == F - 1
    below = jnp.where(first, 0.0, pltpu.roll(amplitude, 1, 1))
    above = jnp.where(last, 0.0, pltpu.roll(amplitude, 2 * F - 1, 1))
    share = jnp.where(first | last, 1.0 / 2.0, 1.0 / 3.0)
    smooth = (below + amplitude + above) * share
    mean = jnp.sum(amplitude, axis=1, keepdims=True) * (0.5 / F)
    level = jnp.maximum(smooth, water_level * (mean + norm_floor))
    taper = jnp.concatenate([taper_ref[...], taper_ref[...]], axis=1)
    white = (spectrum * (taper / level)).astype(jnp.bfloat16)
    floor = lax.broadcasted_iota(jnp.int32, (rows, rows), 0) * src_count
    channel = channel_ref[...]
    pick = (channel >= floor) & (channel < floor + src_count)
    pick = pick.astype(jnp.float32).astype(jnp.bfloat16)
    ordered = jnp.dot(pick, white, preferred_element_type=jnp.float32).astype(jnp.bfloat16)
    return ordered.reshape(src_count, rows // src_count, 2 * F)


def spread_kernel(
    src_count, rcv_count, raw_ref, channel_hbm, taper_hbm, basis_hbm, live_hbm,
    first_ref, second_ref, near_ref,
    x_ref, channel_ref, taper_ref, basis_ref, live_ref, mask_ref, normed_ref, ordered_ref, arrived_ref, own_ref,
    swap_send, swap_recv, block_send, block_recv, pass_send, near_send, near_recv, local_sem,
    load_sem, table_sem,
):
    src, rcv = lax.axis_index("src"), lax.axis_index("rcv")
    windows, rows = x_ref.shape[:2]
    half = own_ref.shape[2]
    block_refs = (first_ref, second_ref)

    def load(w):
        return pltpu.make_async_copy(raw_ref.at[w], x_ref.at[w], load_sem.at[w])

    tables = [
        pltpu.make_async_copy(source, target, table_sem.at[n])
        for n, (source, target) in enumerate(
            [
                (live_hbm, live_ref),
                (channel_hbm, channel_ref),
                (taper_hbm, taper_ref),
                (basis_hbm, basis_ref),
            ]
        )
    ]
    for table in tables:
        table.start()
    load(0).start()
    for w in range(1, windows):
        load(w).start()
    pairs = rcv_count // 2
    row, core = rcv // 2, rcv % 2
    mate = rcv + 1 - 2 * core

    def slot(receiver, holder):
        return (receiver + rcv_count - holder) % rcv_count

    def signal(place):
        pl.semaphore_signal(barrier, inc=1, device_id=place, device_id_type=pl.DeviceIdType.MESH)

    def push(source, target, send_sem, recv_sem, place):
        return pltpu.make_async_remote_copy(
            src_ref=source,
            dst_ref=target,
            send_sem=send_sem,
            recv_sem=recv_sem,
            device_id=place,
            device_id_type=pl.DeviceIdType.MESH,
        )

    barrier = pltpu.get_barrier_semaphore()
    for k in range(1, src_count):
        signal(((src + k) % src_count, rcv))
    for k in range(1, rcv_count):
        signal((src, (rcv + k) % rcv_count))
    takes = (rcv >= 1) & (src + rcv < src_count)

    @pl.when(takes)
    def _():
        for k in range(rcv_count):
            signal((src + rcv, k))

    def swap(w, k):
        target = (src + k) % src_count
        return push(
            ordered_ref.at[w, target],
            arrived_ref.at[w, src],
            swap_send.at[w, k],
            swap_recv.at[w, src],
            (target, rcv),
        )

    def swapped(w, k):
        source = (src + k) % src_count
        return push(
            ordered_ref.at[w, source],
            arrived_ref.at[w, source],
            swap_send.at[w, k],
            swap_recv.at[w, source],
            (source, rcv),
        )

    def share(w, h, k):
        to = mate if k == 0 else ((row + k) % pairs) * 2 + core
        place = slot(to, rcv)
        return push(
            own_ref.at[2 * w + h],
            block_refs[h].at[place, w],
            block_send.at[2 * w + h, k],
            block_recv.at[2 * w + h, place],
            (src, to),
        )

    def shared(w, h, holder):
        place = slot(rcv, holder)
        return push(
            own_ref.at[2 * w + h],
            block_refs[h].at[place, w],
            block_send.at[2 * w + h, 0],
            block_recv.at[2 * w + h, place],
            (src, mate),
        )

    def hand_on(w, h, k):
        holder = ((row + k) % pairs) * 2 + core
        place = slot(mate, holder)
        return push(
            block_refs[h].at[slot(rcv, holder), w],
            block_refs[h].at[place, w],
            pass_send.at[2 * w + h, k],
            block_recv.at[2 * w + h, place],
            (src, mate),
        )

    def near(w, to):
        place = slot(to, rcv)
        return push(
            own_ref.at[2 * w],
            near_ref.at[place, w],
            near_send.at[w, to],
            near_recv.at[w, place],
            (src - to, to),
        )

    def keep(w, h):
        return pltpu.make_async_copy(
            own_ref.at[2 * w + h], block_refs[h].at[0, w], local_sem.at[2 * w + h]
        )

    for table in tables:
        table.wait()
    held = lax.broadcasted_iota(jnp.int32, (rows, rows), 0)
    natural = lax.broadcasted_iota(jnp.int32, (rows, rows), 1)
    part = 2 * half
    pick = natural == (held % part) * src_count + held // part
    pick = jnp.where(pick, live_ref[...].astype(jnp.float32), 0.0).astype(jnp.bfloat16)
    ones = jnp.ones((rows, 2 * F), jnp.bfloat16)
    mask = jnp.dot(pick, ones, preferred_element_type=jnp.float32).astype(jnp.bfloat16)
    mask_ref[...] = mask.reshape(src_count, part, 2 * F)
    for w in range(windows):
        load(w).wait()
        ordered_ref[w] = whiten_window(
            w, src_count, x_ref, channel_ref, taper_ref, basis_ref, normed_ref
        )
        if w == 0:
            pl.semaphore_wait(
                barrier, src_count - 1 + rcv_count - 1 + jnp.minimum(src, rcv_count - 1)
            )
        for k in range(1, src_count):
            swap(w, k).start()

    for w in range(windows):
        for k in range(src_count):
            source = (src + k) % src_count
            if k:
                swapped(w, k).wait_recv()
                value = arrived_ref[w, source]
            else:
                value = ordered_ref[w, source]
            value = value * mask_ref[source]
            own_ref[2 * w, source] = value[:half]
            own_ref[2 * w + 1, source] = value[half:]
        for h in range(2):
            for k in range(pairs):
                share(w, h, (k + 1) % pairs).start()
            if h == 0:
                for to in range(1, rcv_count):
                    pl.when(src >= to)(lambda w=w, to=to: near(w, to).start())
            keep(w, h).start()

    for w in range(windows):
        for h in range(2):
            for k in range(1, pairs):
                shared(w, h, ((row + k) % pairs) * 2 + core).wait_recv()
                hand_on(w, h, k).start()

    for w in range(windows):
        for h in range(2):
            for k in range(pairs):
                shared(w, h, ((row + k) % pairs) * 2 + 1 - core).wait_recv()

        @pl.when(takes)
        def _(w=w):
            for k in range(rcv_count):
                push(
                    own_ref.at[2 * w], near_ref.at[k, w], near_send.at[w, 0], near_recv.at[w, k], (src + rcv, k)
                ).wait_recv()

        for k in range(1, src_count):
            swap(w, k).wait_send()
        for h in range(2):
            for k in range(pairs):
                share(w, h, k).wait_send()
                if k:
                    hand_on(w, h, k).wait_send()
            keep(w, h).wait()
        for to in range(1, rcv_count):
            pl.when(src >= to)(lambda w=w, to=to: near(w, to).wait_send())


def spread(raw_samples, channel_of_row, live_channels, bin_taper, src_count, rcv_count):
    windows, rows, length = raw_samples.shape
    part = rows // src_count
    half = part // 2
    lanes = 2 * F
    hbm = pl.BlockSpec(memory_space=pltpu.HBM)
    anywhere = pl.BlockSpec(memory_space=pl.ANY)
    dma = pltpu.SemaphoreType.DMA
    gathered = jax.ShapeDtypeStruct((rcv_count, windows, src_count, half, lanes), jnp.bfloat16)
    return pl.pallas_call(
        functools.partial(spread_kernel, src_count, rcv_count),
        out_shape=[gathered] * 3,
        in_specs=[hbm] * 5,
        out_specs=[anywhere] * 3,
        scratch_shapes=[
            pltpu.VMEM((windows, rows, length), jnp.bfloat16),
            pltpu.VMEM((1, rows), jnp.int32),
            pltpu.VMEM((1, F), jnp.float32),
            pltpu.VMEM((length, lanes), jnp.bfloat16),
            pltpu.VMEM((1, rows), jnp.int32),
            pltpu.VMEM((src_count, part, lanes), jnp.bfloat16),
            pltpu.VMEM((rows, length), jnp.bfloat16),
            pltpu.VMEM((windows, src_count, part, lanes), jnp.bfloat16),
            pltpu.VMEM((windows, src_count, part, lanes), jnp.bfloat16),
            pltpu.VMEM((2 * windows, src_count, half, lanes), jnp.bfloat16),
            dma((windows, src_count)),
            dma((windows, src_count)),
            dma((2 * windows, rcv_count // 2)),
            dma((2 * windows, rcv_count)),
            dma((2 * windows, rcv_count // 2)),
            dma((windows, rcv_count)),
            dma((windows, rcv_count)),
            dma((2 * windows,)),
            dma((windows,)),
            dma((4,)),
        ],
        compiler_params=pltpu.CompilerParams(
            collective_id=0, has_side_effects=True, vmem_limit_bytes=64 << 20
        ),
        name="spread",
    )(
        raw_samples,
        channel_of_row.reshape(1, rows),
        bin_taper.reshape(1, F),
        jnp.asarray(basis_table(length)),
        live_channels.reshape(1, rows),
    )


def correlate_kernel(pieces, half_index, scale, *refs):
    if half_index:
        own_refs = {1: refs[0]}
        source_ref, *small_refs, left_ref, _, out_ref = refs[1:8]
    else:
        own_refs = dict(enumerate(refs[:2]))
        source_ref, *small_refs, out_ref, left_ref = refs[2:8]
    reach_ref, straight_ref, swapped_ref, small_sem = refs[8:12]
    high_ref, rcv_ref, turned_ref, even_ref, odd_ref = refs[12:]
    step = pl.program_id(0)
    local, src_count, half, lanes = source_ref.shape[1:]
    halves = 2
    windows = pieces * local
    count = src_count * half
    rows = halves * count
    columns = CHUNK * LAGS
    src, rcv = lax.axis_index("src"), lax.axis_index("rcv")

    def rotate(first, target):
        straight = straight_ref[...][None]
        swapped = swapped_ref[...][None]
        for w in range(windows):
            plain = rcv_ref[pl.ds(first, CHUNK), w * lanes : (w + 1) * lanes]
            turned = turned_ref[pl.ds(first, CHUNK), w * lanes : (w + 1) * lanes]
            value = plain[:, None, :] * straight + turned[:, None, :] * swapped
            target[:, w * lanes : (w + 1) * lanes] = value.reshape(columns, lanes).astype(
                jnp.bfloat16
            )

    @pl.when(step == 0)
    def _():
        copies = [
            pltpu.make_async_copy(source, target, small_sem.at[n])
            for n, (source, target) in enumerate(
                zip(small_refs, (reach_ref, straight_ref, swapped_ref))
            )
        ]
        for copy in copies:
            copy.start()
        natural = lax.broadcasted_iota(jnp.int32, (count, count), 0)
        held = lax.broadcasted_iota(jnp.int32, (count, count), 1)
        pick = natural == (held % half) * src_count + held // half
        pick = pick.astype(jnp.float32).astype(jnp.bfloat16)
        for d in range(pieces):
            span = slice(d * local * lanes, (d + 1) * local * lanes)
            own = {
                h: jnp.concatenate([ref[d, n].reshape(count, lanes) for n in range(local)], axis=1)
                for h, ref in own_refs.items()
            }
            if not half_index:
                for h in range(halves):
                    left_ref[h * count : (h + 1) * count, span] = jnp.dot(
                        pick, own[h], preferred_element_type=jnp.float32
                    ).astype(jnp.bfloat16)
            other = jnp.concatenate(
                [source_ref[d, n].reshape(count, lanes) for n in range(local)], axis=1
            )
            block = jnp.where(rcv == 0, own[half_index], other)
            value = jnp.dot(pick, block, preferred_element_type=jnp.float32)
            rcv_ref[:, span] = value
            for n in range(local):
                at = (d * local + n) * lanes
                turned_ref[:, at : at + lanes] = pltpu.roll(
                    value[:, n * lanes : (n + 1) * lanes], F, 1
                )
        for copy in copies:
            copy.wait()
        rotate(0, even_ref)
        row = lax.broadcasted_iota(jnp.int32, (rows, rows), 0)
        column = lax.broadcasted_iota(jnp.int32, (rows, rows), 1)
        reach = jnp.where(row == column, reach_ref[...].astype(jnp.float32), 0.0)
        reach = jnp.sum(reach, axis=1, keepdims=True).astype(jnp.int32)
        first = (lax.broadcasted_iota(jnp.int32, (rows, 1), 0) - rcv * rows) * LAGS
        last = first + reach * LAGS + (LAGS - 1)
        high_ref[...] = jnp.where(src + rcv < src_count, last, -1)

    low = (lax.broadcasted_iota(jnp.int32, (rows, 1), 0) - rcv * rows) * LAGS
    high = high_ref[...]

    def multiply(source, turn):
        total = lax.dot_general(
            left_ref[...], source[...], (((1,), (1,)), ((), ())), preferred_element_type=jnp.float32
        )
        column = lax.broadcasted_iota(jnp.int32, (1, columns), 1)
        column = column + (2 * step + turn) * columns + half_index * count * LAGS
        keep = (column >= low) & (column <= high)
        out_ref[:, turn * columns : (turn + 1) * columns] = jnp.where(
            keep, total * scale, 0.0
        ).astype(jnp.bfloat16)

    rotate((2 * step + 1) * CHUNK, odd_ref)
    multiply(even_ref, 0)
    rotate(jnp.minimum(2 * step + 2, count // CHUNK - 1) * CHUNK, even_ref)
    multiply(odd_ref, 1)


def correlate(blocks, receivers, band_reach, length, earlier=None):
    half_index = int(earlier is not None)
    pieces, local, src_count, half, lanes = receivers.shape
    halves = 2
    count = src_count * half
    rows = halves * count
    windows = pieces * local
    depth = windows * lanes
    columns = CHUNK * LAGS
    steps = count // (2 * CHUNK)
    straight, swapped = lag_tables(length)
    whole = lambda *shape: pl.BlockSpec(shape, lambda g: (0,) * len(shape))
    operands = [
        *blocks, receivers, band_reach.reshape(1, rows), jnp.asarray(straight), jnp.asarray(swapped)
    ]
    in_specs = [whole(*operand.shape) for operand in operands]
    in_specs[-3:] = [pl.BlockSpec(memory_space=pltpu.HBM)] * 3
    out_shape = [jax.ShapeDtypeStruct((rows, rows * LAGS), jnp.bfloat16)]
    out_specs = [pl.BlockSpec((rows, 2 * columns), lambda g: (0, g + half_index * steps))]
    aliases = {}
    if half_index:
        operands += [earlier[1], earlier[0]]
        in_specs += [whole(rows, depth), pl.BlockSpec(memory_space=pl.ANY)]
        aliases = {len(operands) - 1: 0}
    else:
        out_shape.append(jax.ShapeDtypeStruct((rows, depth), jnp.bfloat16))
        out_specs.append(whole(rows, depth))
    return pl.pallas_call(
        functools.partial(correlate_kernel, pieces, half_index, 1.0 / math.sqrt(windows)),
        grid=(steps,),
        out_shape=out_shape,
        in_specs=in_specs,
        out_specs=out_specs,
        scratch_shapes=[
            pltpu.VMEM((1, rows), jnp.int32),
            pltpu.VMEM((LAGS, lanes), jnp.float32),
            pltpu.VMEM((LAGS, lanes), jnp.float32),
            pltpu.SemaphoreType.DMA((3,)),
            pltpu.VMEM((rows, 1), jnp.int32),
            pltpu.VMEM((count, depth), jnp.float32),
            pltpu.VMEM((count, depth), jnp.float32),
            pltpu.VMEM((columns, depth), jnp.bfloat16),
            pltpu.VMEM((columns, depth), jnp.bfloat16),
        ],
        input_output_aliases=aliases,
        cost_estimate=pl.CostEstimate(
            flops=2 * rows * depth * count * LAGS,
            bytes_accessed=2 * rows * count * LAGS,
            transcendentals=0,
        ),
        compiler_params=pltpu.CompilerParams(vmem_limit_bytes=64 << 20),
        name="correlate",
    )(*operands)


def body(raw_samples, channel_of_row, live_channels, band_reach, bin_taper):
    src_count = lax.axis_size("src")
    rcv_count = lax.axis_size("rcv")
    length = raw_samples.shape[2]
    first, second, near = spread(
        raw_samples, channel_of_row, live_channels, bin_taper, src_count, rcv_count
    )
    route = []
    for s in range(src_count):
        for to in range(1, rcv_count):
            if s >= to:
                route.append((s * rcv_count + to, (s - to) * rcv_count + to))
    far = lax.ppermute(second, ("src", "rcv"), route)
    earlier = correlate([first, second], near, band_reach, length)
    return correlate([second], far, band_reach, length, earlier)[0]


def solution(mesh):
    return jax.shard_map(
        body,
        mesh=mesh,
        in_specs=(P("rcv", "src", None), P("src"), P("src"), P("src"), P()),
        out_specs=P("src", "rcv"),
        check_vma=False,
    )
```

```python
import functools
import math

import jax
import jax.numpy as jnp
import ml_dtypes
import numpy as np
from jax import lax
from jax.experimental import pallas as pl
from jax.experimental.pallas import tpu as pltpu
from jax.sharding import PartitionSpec as P

F = 64
K0 = 32
HW = 64
LAGS = 32
CHUNK = 16

norm_floor = 1e-05
water_level = 0.3


def basis_table(length):
    sample_index = np.arange(length)
    bin_index = np.arange(F) + K0
    phase = np.mod(sample_index[:, None] * bin_index[None, :], length)
    angle = phase * (2.0 * math.pi / length)
    table = np.concatenate([np.cos(angle), -np.sin(angle)], axis=1)
    return table.astype(np.float32).astype(ml_dtypes.bfloat16)


def lag_tables(length):
    bin_index = np.arange(F) + K0
    lag_index = np.arange(LAGS) - LAGS // 2
    phase = np.mod(lag_index[:, None] * bin_index[None, :], length)
    angle = phase * (2.0 * math.pi / length)
    scale = 1.0 / math.sqrt(F)
    cosine = (np.cos(angle) * scale).astype(np.float32).astype(ml_dtypes.bfloat16)
    sine = (np.sin(angle) * scale).astype(np.float32).astype(ml_dtypes.bfloat16)
    straight = np.concatenate([cosine, cosine], axis=1).astype(np.float32)
    swapped = np.concatenate([-sine, sine], axis=1).astype(np.float32)
    return straight, swapped


def inverse_counts(start, width, length):
    position = lax.broadcasted_iota(jnp.int32, (1, width), 1) + start
    upper = jnp.minimum(position + HW, length - 1)
    lower = jnp.maximum(position - HW, 0)
    return 1.0 / (upper - lower + 1).astype(jnp.float32)


def band(rows, columns, shift):
    row = lax.broadcasted_iota(jnp.int32, (rows, columns), 0)
    column = lax.broadcasted_iota(jnp.int32, (rows, columns), 1)
    return (jnp.abs(row - column - shift) <= HW).astype(jnp.float32).astype(jnp.bfloat16)


def whiten_window(w, src_count, x_ref, channel_ref, taper_ref, basis_ref, normed_ref):
    rows, length = x_ref.shape[1:]
    width = 256
    for start in range(0, length, width):
        low = max(start - 128, 0)
        high = min(start + width + 128, length)
        magnitude = jnp.abs(x_ref[w, :, low:high])
        total = jnp.dot(
            magnitude, band(high - low, width, start - low), preferred_element_type=jnp.float32
        )
        level = total * inverse_counts(start, width, length) + norm_floor
        values = x_ref[w, :, start : start + width].astype(jnp.float32)
        normed_ref[:, start : start + width] = (values / level).astype(jnp.bfloat16)
    spectrum = jnp.dot(normed_ref[...], basis_ref[...], preferred_element_type=jnp.float32)
    square = spectrum * spectrum
    amplitude = jnp.sqrt(square + pltpu.roll(square, F, 1))
    bins = lax.broadcasted_iota(jnp.int32, (1, 2 * F), 1) % F
    first, last = bins == 0, bins == F - 1
    below = jnp.where(first, 0.0, pltpu.roll(amplitude, 1, 1))
    above = jnp.where(last, 0.0, pltpu.roll(amplitude, 2 * F - 1, 1))
    share = jnp.where(first | last, 1.0 / 2.0, 1.0 / 3.0)
    smooth = (below + amplitude + above) * share
    mean = jnp.sum(amplitude, axis=1, keepdims=True) * (0.5 / F)
    level = jnp.maximum(smooth, water_level * (mean + norm_floor))
    taper = jnp.concatenate([taper_ref[...], taper_ref[...]], axis=1)
    white = (spectrum * (taper / level)).astype(jnp.bfloat16)
    floor = lax.broadcasted_iota(jnp.int32, (rows, rows), 0) * src_count
    channel = channel_ref[...]
    pick = (channel >= floor) & (channel < floor + src_count)
    pick = pick.astype(jnp.float32).astype(jnp.bfloat16)
    ordered = jnp.dot(pick, white, preferred_element_type=jnp.float32).astype(jnp.bfloat16)
    return ordered.reshape(src_count, rows // src_count, 2 * F)


def spread_kernel(
    src_count, rcv_count, raw_ref, channel_hbm, taper_hbm, basis_hbm, live_hbm,
    first_ref, second_ref, near_ref,
    x_ref, channel_ref, taper_ref, basis_ref, live_ref, mask_ref, normed_ref, ordered_ref, arrived_ref, own_ref,
    swap_send, swap_recv, block_send, block_recv, pass_send, near_send, near_recv, relay_send, local_sem,
    load_sem, table_sem,
):
    src, rcv = lax.axis_index("src"), lax.axis_index("rcv")
    windows, rows = x_ref.shape[:2]
    half = own_ref.shape[2]
    block_refs = (first_ref, second_ref)

    def load(w):
        return pltpu.make_async_copy(raw_ref.at[w], x_ref.at[w], load_sem.at[w])

    tables = [
        pltpu.make_async_copy(source, target, table_sem.at[n])
        for n, (source, target) in enumerate(
            [
                (live_hbm, live_ref),
                (channel_hbm, channel_ref),
                (taper_hbm, taper_ref),
                (basis_hbm, basis_ref),
            ]
        )
    ]
    for table in tables:
        table.start()
    load(0).start()
    for w in range(1, windows):
        load(w).start()
    pairs = rcv_count // 2
    row, core = rcv // 2, rcv % 2
    mate = rcv + 1 - 2 * core

    def signal(place):
        pl.semaphore_signal(barrier, inc=1, device_id=place, device_id_type=pl.DeviceIdType.MESH)

    def push(source, target, send_sem, recv_sem, place):
        return pltpu.make_async_remote_copy(
            src_ref=source,
            dst_ref=target,
            send_sem=send_sem,
            recv_sem=recv_sem,
            device_id=place,
            device_id_type=pl.DeviceIdType.MESH,
        )

    barrier = pltpu.get_barrier_semaphore()
    for k in range(1, src_count):
        signal(((src + k) % src_count, rcv))
    for k in range(1, rcv_count):
        signal((src, (rcv + k) % rcv_count))
    takes = (rcv >= 1) & (src + rcv < src_count)

    relayed = (rcv >= 3) & (core == 1)
    relays = takes & (rcv >= 2) & (core == 0) & (src >= 1)
    direct = [to for to in range(1, rcv_count) if to == 1 or to % 2 == 0]

    @pl.when(takes & jnp.logical_not(relayed))
    def _():
        for k in range(rcv_count):
            signal((src + rcv, k))

    @pl.when(takes & relayed)
    def _():
        signal((src + 1, rcv - 1))

    def swap(w, k):
        target = (src + k) % src_count
        return push(
            ordered_ref.at[w, target],
            arrived_ref.at[w, src],
            swap_send.at[w, k],
            swap_recv.at[w, src],
            (target, rcv),
        )

    def swapped(w, k):
        source = (src + k) % src_count
        return push(
            ordered_ref.at[w, source],
            arrived_ref.at[w, source],
            swap_send.at[w, k],
            swap_recv.at[w, source],
            (source, rcv),
        )

    def share(w, h, k):
        to = mate if k == 0 else ((row + k) % pairs) * 2 + core
        return push(
            own_ref.at[2 * w + h],
            block_refs[h].at[rcv, w],
            block_send.at[2 * w + h, k],
            block_recv.at[2 * w + h, rcv],
            (src, to),
        )

    def shared(w, h, holder):
        return push(
            own_ref.at[2 * w + h],
            block_refs[h].at[holder, w],
            block_send.at[2 * w + h, 0],
            block_recv.at[2 * w + h, holder],
            (src, mate),
        )

    def hand_on(w, h, k):
        holder = ((row + k) % pairs) * 2 + core
        return push(
            block_refs[h].at[holder, w],
            block_refs[h].at[holder, w],
            pass_send.at[2 * w + h, k],
            block_recv.at[2 * w + h, holder],
            (src, mate),
        )

    def near(w, to):
        return push(
            own_ref.at[2 * w],
            near_ref.at[rcv, w],
            near_send.at[w, to],
            near_recv.at[w, rcv],
            (src - to, to),
        )

    def relay(w, k):
        return push(
            near_ref.at[k, w],
            near_ref.at[k, w],
            relay_send.at[w, k],
            near_recv.at[w, k],
            (src - 1, rcv + 1),
        )

    def keep(w, h):
        return pltpu.make_async_copy(
            own_ref.at[2 * w + h], block_refs[h].at[rcv, w], local_sem.at[2 * w + h]
        )

    for table in tables:
        table.wait()
    held = lax.broadcasted_iota(jnp.int32, (rows, rows), 0)
    natural = lax.broadcasted_iota(jnp.int32, (rows, rows), 1)
    part = 2 * half
    pick = natural == (held % part) * src_count + held // part
    pick = jnp.where(pick, live_ref[...].astype(jnp.float32), 0.0).astype(jnp.bfloat16)
    ones = jnp.ones((rows, 2 * F), jnp.bfloat16)
    mask = jnp.dot(pick, ones, preferred_element_type=jnp.float32).astype(jnp.bfloat16)
    mask_ref[...] = mask.reshape(src_count, part, 2 * F)
    for w in range(windows):
        load(w).wait()
        ordered_ref[w] = whiten_window(
            w, src_count, x_ref, channel_ref, taper_ref, basis_ref, normed_ref
        )
        if w == 0:
            expected = src_count - 1 + rcv_count - 1 + jnp.where(relays, 1, 0)
            for to in direct:
                expected = expected + jnp.where(src >= to, 1, 0)
            pl.semaphore_wait(barrier, expected)
        for k in range(1, src_count):
            swap(w, k).start()

    for w in range(windows):
        for k in range(src_count):
            source = (src + k) % src_count
            if k:
                swapped(w, k).wait_recv()
                value = arrived_ref[w, source]
            else:
                value = ordered_ref[w, source]
            value = value * mask_ref[source]
            own_ref[2 * w, source] = value[:half]
            own_ref[2 * w + 1, source] = value[half:]
        for h in range(2):
            for k in range(pairs):
                share(w, h, (k + 1) % pairs).start()
            if h == 0:
                for to in direct:
                    pl.when(src >= to)(lambda w=w, to=to: near(w, to).start())
            keep(w, h).start()

    for w in range(windows):
        for h in range(2):
            for k in range(1, pairs):
                shared(w, h, ((row + k) % pairs) * 2 + core).wait_recv()
                hand_on(w, h, k).start()

    for w in range(windows):
        for k in range(rcv_count):
            arrival = push(
                near_ref.at[k, w], near_ref.at[k, w], near_send.at[w, 0], near_recv.at[w, k], (src, mate)
            )
            pl.when(takes)(lambda arrival=arrival: arrival.wait_recv())
            pl.when(relays)(lambda w=w, k=k: relay(w, k).start())

    for w in range(windows):
        for h in range(2):
            for k in range(pairs):
                shared(w, h, ((row + k) % pairs) * 2 + 1 - core).wait_recv()

        for k in range(1, src_count):
            swap(w, k).wait_send()
        for h in range(2):
            for k in range(pairs):
                share(w, h, k).wait_send()
                if k:
                    hand_on(w, h, k).wait_send()
            keep(w, h).wait()
        for to in direct:
            pl.when(src >= to)(lambda w=w, to=to: near(w, to).wait_send())

        @pl.when(relays)
        def _(w=w):
            for k in range(rcv_count):
                relay(w, k).wait_send()


def spread(raw_samples, channel_of_row, live_channels, bin_taper, src_count, rcv_count):
    windows, rows, length = raw_samples.shape
    part = rows // src_count
    half = part // 2
    lanes = 2 * F
    hbm = pl.BlockSpec(memory_space=pltpu.HBM)
    anywhere = pl.BlockSpec(memory_space=pl.ANY)
    dma = pltpu.SemaphoreType.DMA
    gathered = jax.ShapeDtypeStruct((rcv_count, windows, src_count, half, lanes), jnp.bfloat16)
    return pl.pallas_call(
        functools.partial(spread_kernel, src_count, rcv_count),
        out_shape=[gathered] * 3,
        in_specs=[hbm] * 5,
        out_specs=[anywhere] * 3,
        scratch_shapes=[
            pltpu.VMEM((windows, rows, length), jnp.bfloat16),
            pltpu.VMEM((1, rows), jnp.int32),
            pltpu.VMEM((1, F), jnp.float32),
            pltpu.VMEM((length, lanes), jnp.bfloat16),
            pltpu.VMEM((1, rows), jnp.int32),
            pltpu.VMEM((src_count, part, lanes), jnp.bfloat16),
            pltpu.VMEM((rows, length), jnp.bfloat16),
            pltpu.VMEM((windows, src_count, part, lanes), jnp.bfloat16),
            pltpu.VMEM((windows, src_count, part, lanes), jnp.bfloat16),
            pltpu.VMEM((2 * windows, src_count, half, lanes), jnp.bfloat16),
            dma((windows, src_count)),
            dma((windows, src_count)),
            dma((2 * windows, rcv_count // 2)),
            dma((2 * windows, rcv_count)),
            dma((2 * windows, rcv_count // 2)),
            dma((windows, rcv_count)),
            dma((windows, rcv_count)),
            dma((windows, rcv_count)),
            dma((2 * windows,)),
            dma((windows,)),
            dma((4,)),
        ],
        compiler_params=pltpu.CompilerParams(
            collective_id=0, has_side_effects=True, vmem_limit_bytes=64 << 20
        ),
        name="spread",
    )(
        raw_samples,
        channel_of_row.reshape(1, rows),
        bin_taper.reshape(1, F),
        jnp.asarray(basis_table(length)),
        live_channels.reshape(1, rows),
    )


def correlate_kernel(pieces, half_index, scale, *refs):
    if half_index:
        own_refs = {1: refs[0]}
        source_ref, *small_refs, left_ref, _, out_ref = refs[1:8]
    else:
        own_refs = dict(enumerate(refs[:2]))
        source_ref, *small_refs, out_ref, left_ref = refs[2:8]
    reach_ref, straight_ref, swapped_ref, small_sem = refs[8:12]
    high_ref, rcv_ref, turned_ref, even_ref, odd_ref = refs[12:]
    step = pl.program_id(0)
    local, src_count, half, lanes = source_ref.shape[1:]
    halves = 2
    windows = pieces * local
    count = src_count * half
    rows = halves * count
    columns = CHUNK * LAGS
    src, rcv = lax.axis_index("src"), lax.axis_index("rcv")

    def rotate(first, target):
        straight = straight_ref[...][None]
        swapped = swapped_ref[...][None]
        for w in range(windows):
            plain = rcv_ref[pl.ds(first, CHUNK), w * lanes : (w + 1) * lanes]
            turned = turned_ref[pl.ds(first, CHUNK), w * lanes : (w + 1) * lanes]
            value = plain[:, None, :] * straight + turned[:, None, :] * swapped
            target[:, w * lanes : (w + 1) * lanes] = value.reshape(columns, lanes).astype(
                jnp.bfloat16
            )

    @pl.when(step == 0)
    def _():
        copies = [
            pltpu.make_async_copy(source, target, small_sem.at[n])
            for n, (source, target) in enumerate(
                zip(small_refs, (reach_ref, straight_ref, swapped_ref))
            )
        ]
        for copy in copies:
            copy.start()
        natural = lax.broadcasted_iota(jnp.int32, (count, count), 0)
        held = lax.broadcasted_iota(jnp.int32, (count, count), 1)
        pick = natural == (held % half) * src_count + held // half
        pick = pick.astype(jnp.float32).astype(jnp.bfloat16)
        for d in range(pieces):
            span = slice(d * local * lanes, (d + 1) * local * lanes)
            own = {
                h: jnp.concatenate([ref[d, n].reshape(count, lanes) for n in range(local)], axis=1)
                for h, ref in own_refs.items()
            }
            if not half_index:
                for h in range(halves):
                    left_ref[h * count : (h + 1) * count, span] = jnp.dot(
                        pick, own[h], preferred_element_type=jnp.float32
                    ).astype(jnp.bfloat16)
            other = jnp.concatenate(
                [source_ref[d, n].reshape(count, lanes) for n in range(local)], axis=1
            )
            block = jnp.where(rcv == 0, own[half_index], other)
            value = jnp.dot(pick, block, preferred_element_type=jnp.float32)
            rcv_ref[:, span] = value
            for n in range(local):
                at = (d * local + n) * lanes
                turned_ref[:, at : at + lanes] = pltpu.roll(
                    value[:, n * lanes : (n + 1) * lanes], F, 1
                )
        for copy in copies:
            copy.wait()
        rotate(0, even_ref)
        row = lax.broadcasted_iota(jnp.int32, (rows, rows), 0)
        column = lax.broadcasted_iota(jnp.int32, (rows, rows), 1)
        reach = jnp.where(row == column, reach_ref[...].astype(jnp.float32), 0.0)
        reach = jnp.sum(reach, axis=1, keepdims=True).astype(jnp.int32)
        first = (lax.broadcasted_iota(jnp.int32, (rows, 1), 0) - rcv * rows) * LAGS
        last = first + reach * LAGS + (LAGS - 1)
        high_ref[...] = jnp.where(src + rcv < src_count, last, -1)

    low = (lax.broadcasted_iota(jnp.int32, (rows, 1), 0) - rcv * rows) * LAGS
    high = high_ref[...]

    def multiply(source, turn):
        total = lax.dot_general(
            left_ref[...], source[...], (((1,), (1,)), ((), ())), preferred_element_type=jnp.float32
        )
        column = lax.broadcasted_iota(jnp.int32, (1, columns), 1)
        column = column + (2 * step + turn) * columns + half_index * count * LAGS
        keep = (column >= low) & (column <= high)
        out_ref[:, turn * columns : (turn + 1) * columns] = jnp.where(
            keep, total * scale, 0.0
        ).astype(jnp.bfloat16)

    rotate((2 * step + 1) * CHUNK, odd_ref)
    multiply(even_ref, 0)
    rotate(jnp.minimum(2 * step + 2, count // CHUNK - 1) * CHUNK, even_ref)
    multiply(odd_ref, 1)


def correlate(blocks, receivers, band_reach, length, earlier=None):
    half_index = int(earlier is not None)
    pieces, local, src_count, half, lanes = receivers.shape
    halves = 2
    count = src_count * half
    rows = halves * count
    windows = pieces * local
    depth = windows * lanes
    columns = CHUNK * LAGS
    steps = count // (2 * CHUNK)
    straight, swapped = lag_tables(length)
    whole = lambda *shape: pl.BlockSpec(shape, lambda g: (0,) * len(shape))
    operands = [
        *blocks, receivers, band_reach.reshape(1, rows), jnp.asarray(straight), jnp.asarray(swapped)
    ]
    in_specs = [whole(*operand.shape) for operand in operands]
    in_specs[-3:] = [pl.BlockSpec(memory_space=pltpu.HBM)] * 3
    out_shape = [jax.ShapeDtypeStruct((rows, rows * LAGS), jnp.bfloat16)]
    out_specs = [pl.BlockSpec((rows, 2 * columns), lambda g: (0, g + half_index * steps))]
    aliases = {}
    if half_index:
        operands += [earlier[1], earlier[0]]
        in_specs += [whole(rows, depth), pl.BlockSpec(memory_space=pl.ANY)]
        aliases = {len(operands) - 1: 0}
    else:
        out_shape.append(jax.ShapeDtypeStruct((rows, depth), jnp.bfloat16))
        out_specs.append(whole(rows, depth))
    return pl.pallas_call(
        functools.partial(correlate_kernel, pieces, half_index, 1.0 / math.sqrt(windows)),
        grid=(steps,),
        out_shape=out_shape,
        in_specs=in_specs,
        out_specs=out_specs,
        scratch_shapes=[
            pltpu.VMEM((1, rows), jnp.int32),
            pltpu.VMEM((LAGS, lanes), jnp.float32),
            pltpu.VMEM((LAGS, lanes), jnp.float32),
            pltpu.SemaphoreType.DMA((3,)),
            pltpu.VMEM((rows, 1), jnp.int32),
            pltpu.VMEM((count, depth), jnp.float32),
            pltpu.VMEM((count, depth), jnp.float32),
            pltpu.VMEM((columns, depth), jnp.bfloat16),
            pltpu.VMEM((columns, depth), jnp.bfloat16),
        ],
        input_output_aliases=aliases,
        cost_estimate=pl.CostEstimate(
            flops=2 * rows * depth * count * LAGS,
            bytes_accessed=2 * rows * count * LAGS,
            transcendentals=0,
        ),
        compiler_params=pltpu.CompilerParams(vmem_limit_bytes=64 << 20),
        name="correlate",
    )(*operands)


def body(raw_samples, channel_of_row, live_channels, band_reach, bin_taper):
    src_count = lax.axis_size("src")
    rcv_count = lax.axis_size("rcv")
    length = raw_samples.shape[2]
    first, second, near = spread(
        raw_samples, channel_of_row, live_channels, bin_taper, src_count, rcv_count
    )
    route = []
    for s in range(src_count):
        for to in range(1, rcv_count):
            if s >= to:
                holder = to if to < 3 or to % 2 == 0 else (to - 2 if to > 3 else 0)
                route.append((s * rcv_count + holder, (s - to) * rcv_count + to))
    far = lax.ppermute(second, ("src", "rcv"), route)
    earlier = correlate([first, second], near, band_reach, length)
    return correlate([second], far, band_reach, length, earlier)[0]


def solution(mesh):
    return jax.shard_map(
        body,
        mesh=mesh,
        in_specs=(P("rcv", "src", None), P("src"), P("src"), P("src"), P()),
        out_specs=P("src", "rcv"),
        check_vma=False,
    )
```

```python
import functools
import math

import jax
import jax.numpy as jnp
import ml_dtypes
import numpy as np
from jax import lax
from jax.experimental import pallas as pl
from jax.experimental.pallas import tpu as pltpu
from jax.sharding import PartitionSpec as P

F = 64
K0 = 32
HW = 64
LAGS = 32
CHUNK = 16
GROUP = 16

norm_floor = 1e-05
water_level = 0.3


def basis_table(length):
    sample_index = np.arange(length)
    bin_index = np.arange(F) + K0
    phase = np.mod(sample_index[:, None] * bin_index[None, :], length)
    angle = phase * (2.0 * math.pi / length)
    table = np.concatenate([np.cos(angle), -np.sin(angle)], axis=1)
    return table.astype(np.float32).astype(ml_dtypes.bfloat16)


def lag_tables(length):
    bin_index = np.arange(F) + K0
    lag_index = np.arange(LAGS) - LAGS // 2
    phase = np.mod(lag_index[:, None] * bin_index[None, :], length)
    angle = phase * (2.0 * math.pi / length)
    scale = 1.0 / math.sqrt(F)
    cosine = (np.cos(angle) * scale).astype(np.float32).astype(ml_dtypes.bfloat16)
    sine = (np.sin(angle) * scale).astype(np.float32).astype(ml_dtypes.bfloat16)
    straight = np.concatenate([cosine, cosine], axis=1)
    swapped = np.concatenate([-sine, sine], axis=1)
    return straight, swapped


def inverse_counts(start, width, length):
    position = lax.broadcasted_iota(jnp.int32, (1, width), 1) + start
    upper = jnp.minimum(position + HW, length - 1)
    lower = jnp.maximum(position - HW, 0)
    return 1.0 / (upper - lower + 1).astype(jnp.float32)


def band(rows, columns, shift):
    row = lax.broadcasted_iota(jnp.int32, (rows, columns), 0)
    column = lax.broadcasted_iota(jnp.int32, (rows, columns), 1)
    return (jnp.abs(row - column - shift) <= HW).astype(jnp.float32).astype(jnp.bfloat16)


def whiten_window(w, src_count, x_ref, channel_ref, taper_ref, basis_ref, normed_ref):
    rows, length = x_ref.shape[1:]
    width = 256
    for start in range(0, length, width):
        low = max(start - 128, 0)
        high = min(start + width + 128, length)
        magnitude = jnp.abs(x_ref[w, :, low:high])
        total = jnp.dot(
            magnitude, band(high - low, width, start - low), preferred_element_type=jnp.float32
        )
        level = total * inverse_counts(start, width, length) + norm_floor
        values = x_ref[w, :, start : start + width].astype(jnp.float32)
        normed_ref[:, start : start + width] = (values / level).astype(jnp.bfloat16)
    spectrum = jnp.dot(normed_ref[...], basis_ref[...], preferred_element_type=jnp.float32)
    square = spectrum * spectrum
    amplitude = jnp.sqrt(square + pltpu.roll(square, F, 1))
    bins = lax.broadcasted_iota(jnp.int32, (1, 2 * F), 1) % F
    first, last = bins == 0, bins == F - 1
    below = jnp.where(first, 0.0, pltpu.roll(amplitude, 1, 1))
    above = jnp.where(last, 0.0, pltpu.roll(amplitude, 2 * F - 1, 1))
    share = jnp.where(first | last, 1.0 / 2.0, 1.0 / 3.0)
    smooth = (below + amplitude + above) * share
    mean = jnp.sum(amplitude, axis=1, keepdims=True) * (0.5 / F)
    level = jnp.maximum(smooth, water_level * (mean + norm_floor))
    taper = jnp.concatenate([taper_ref[...], taper_ref[...]], axis=1)
    white = (spectrum * (taper / level)).astype(jnp.bfloat16)
    floor = lax.broadcasted_iota(jnp.int32, (rows, rows), 0) * src_count
    channel = channel_ref[...]
    pick = (channel >= floor) & (channel < floor + src_count)
    pick = pick.astype(jnp.float32).astype(jnp.bfloat16)
    ordered = jnp.dot(pick, white, preferred_element_type=jnp.float32).astype(jnp.bfloat16)
    return ordered.reshape(src_count, rows // src_count, 2 * F)


def spread_kernel(
    src_count, rcv_count, raw_ref, channel_hbm, taper_hbm, basis_hbm, live_hbm,
    first_ref, second_ref, near_ref,
    x_ref, channel_ref, taper_ref, basis_ref, live_ref, mask_ref, normed_ref, ordered_ref, arrived_ref, own_ref,
    swap_send, swap_recv, block_send, block_recv, pass_send, near_send, near_recv, local_sem,
    load_sem, table_sem,
):
    src, rcv = lax.axis_index("src"), lax.axis_index("rcv")
    windows, rows = x_ref.shape[:2]
    half = own_ref.shape[2]
    block_refs = (first_ref, second_ref)

    def load(w):
        return pltpu.make_async_copy(raw_ref.at[w], x_ref.at[w], load_sem.at[w])

    tables = [
        pltpu.make_async_copy(source, target, table_sem.at[n])
        for n, (source, target) in enumerate(
            [
                (live_hbm, live_ref),
                (channel_hbm, channel_ref),
                (taper_hbm, taper_ref),
                (basis_hbm, basis_ref),
            ]
        )
    ]
    for table in tables:
        table.start()
    load(0).start()
    for w in range(1, windows):
        load(w).start()
    pairs = rcv_count // 2
    row, core = rcv // 2, rcv % 2
    mate = rcv + 1 - 2 * core

    def signal(place):
        pl.semaphore_signal(barrier, inc=1, device_id=place, device_id_type=pl.DeviceIdType.MESH)

    def push(source, target, send_sem, recv_sem, place):
        return pltpu.make_async_remote_copy(
            src_ref=source,
            dst_ref=target,
            send_sem=send_sem,
            recv_sem=recv_sem,
            device_id=place,
            device_id_type=pl.DeviceIdType.MESH,
        )

    barrier = pltpu.get_barrier_semaphore()
    for k in range(1, src_count):
        signal(((src + k) % src_count, rcv))
    for k in range(1, rcv_count):
        signal((src, (rcv + k) % rcv_count))
    takes = (rcv >= 1) & (src + rcv < src_count)

    direct = list(range(rcv_count - 1, 0, -1))

    @pl.when(takes)
    def _():
        for k in range(rcv_count):
            signal((src + rcv, k))

    def swap(w, k):
        target = (src + k) % src_count
        return push(
            ordered_ref.at[w, target],
            arrived_ref.at[w, src],
            swap_send.at[w, k],
            swap_recv.at[w, src],
            (target, rcv),
        )

    def swapped(w, k):
        source = (src + k) % src_count
        return push(
            ordered_ref.at[w, source],
            arrived_ref.at[w, source],
            swap_send.at[w, k],
            swap_recv.at[w, source],
            (source, rcv),
        )

    def share(w, h, k):
        to = mate if k == 0 else ((row + k) % pairs) * 2 + core
        return push(
            own_ref.at[2 * w + h],
            block_refs[h].at[rcv, w],
            block_send.at[2 * w + h, k],
            block_recv.at[2 * w + h, rcv],
            (src, to),
        )

    def shared(w, h, holder):
        return push(
            own_ref.at[2 * w + h],
            block_refs[h].at[holder, w],
            block_send.at[2 * w + h, 0],
            block_recv.at[2 * w + h, holder],
            (src, mate),
        )

    def hand_on(w, h, k):
        holder = ((row + k) % pairs) * 2 + core
        return push(
            block_refs[h].at[holder, w],
            block_refs[h].at[holder, w],
            pass_send.at[2 * w + h, k],
            block_recv.at[2 * w + h, holder],
            (src, mate),
        )

    def near(w, to):
        return push(
            own_ref.at[2 * w],
            near_ref.at[rcv, w],
            near_send.at[w, to],
            near_recv.at[w, rcv],
            (src - to, to),
        )

    def keep(w, h):
        return pltpu.make_async_copy(
            own_ref.at[2 * w + h], block_refs[h].at[rcv, w], local_sem.at[2 * w + h]
        )

    for table in tables:
        table.wait()
    held = lax.broadcasted_iota(jnp.int32, (rows, rows), 0)
    natural = lax.broadcasted_iota(jnp.int32, (rows, rows), 1)
    part = 2 * half
    pick = natural == (held % part) * src_count + held // part
    pick = jnp.where(pick, live_ref[...].astype(jnp.float32), 0.0).astype(jnp.bfloat16)
    ones = jnp.ones((rows, 2 * F), jnp.bfloat16)
    mask = jnp.dot(pick, ones, preferred_element_type=jnp.float32).astype(jnp.bfloat16)
    mask_ref[...] = mask.reshape(src_count, part, 2 * F)
    for w in range(windows):
        load(w).wait()
        ordered_ref[w] = whiten_window(
            w, src_count, x_ref, channel_ref, taper_ref, basis_ref, normed_ref
        )
        if w == 0:
            expected = src_count - 1 + rcv_count - 1
            for to in direct:
                expected = expected + jnp.where(src >= to, 1, 0)
            pl.semaphore_wait(barrier, expected)
        for k in range(1, src_count):
            swap(w, k).start()

    for w in range(windows):
        for k in range(src_count):
            source = (src + k) % src_count
            if k:
                swapped(w, k).wait_recv()
                value = arrived_ref[w, source]
            else:
                value = ordered_ref[w, source]
            value = value * mask_ref[source]
            own_ref[2 * w, source] = value[:half]
            own_ref[2 * w + 1, source] = value[half:]
        for h in range(2):
            for k in range(pairs):
                share(w, h, (k + 1) % pairs).start()
            if h == 0:
                for to in direct:
                    pl.when(src >= to)(lambda w=w, to=to: near(w, to).start())
            keep(w, h).start()

    for w in range(windows):
        for h in range(2):
            for k in range(1, pairs):
                shared(w, h, ((row + k) % pairs) * 2 + core).wait_recv()
                hand_on(w, h, k).start()

    for w in range(windows):
        for k in range(rcv_count):
            arrival = push(
                near_ref.at[k, w], near_ref.at[k, w], near_send.at[w, 0], near_recv.at[w, k], (src, mate)
            )
            pl.when(takes)(lambda arrival=arrival: arrival.wait_recv())

    for w in range(windows):
        for h in range(2):
            for k in range(pairs):
                shared(w, h, ((row + k) % pairs) * 2 + 1 - core).wait_recv()

        for k in range(1, src_count):
            swap(w, k).wait_send()
        for h in range(2):
            for k in range(pairs):
                share(w, h, k).wait_send()
                if k:
                    hand_on(w, h, k).wait_send()
            keep(w, h).wait()
        for to in direct:
            pl.when(src >= to)(lambda w=w, to=to: near(w, to).wait_send())


def spread(raw_samples, channel_of_row, live_channels, bin_taper, src_count, rcv_count):
    windows, rows, length = raw_samples.shape
    part = rows // src_count
    half = part // 2
    lanes = 2 * F
    hbm = pl.BlockSpec(memory_space=pltpu.HBM)
    anywhere = pl.BlockSpec(memory_space=pl.ANY)
    dma = pltpu.SemaphoreType.DMA
    gathered = jax.ShapeDtypeStruct((rcv_count, windows, src_count, half, lanes), jnp.bfloat16)
    return pl.pallas_call(
        functools.partial(spread_kernel, src_count, rcv_count),
        out_shape=[gathered] * 3,
        in_specs=[hbm] * 5,
        out_specs=[anywhere] * 3,
        scratch_shapes=[
            pltpu.VMEM((windows, rows, length), jnp.bfloat16),
            pltpu.VMEM((1, rows), jnp.int32),
            pltpu.VMEM((1, F), jnp.float32),
            pltpu.VMEM((length, lanes), jnp.bfloat16),
            pltpu.VMEM((1, rows), jnp.int32),
            pltpu.VMEM((src_count, part, lanes), jnp.bfloat16),
            pltpu.VMEM((rows, length), jnp.bfloat16),
            pltpu.VMEM((windows, src_count, part, lanes), jnp.bfloat16),
            pltpu.VMEM((windows, src_count, part, lanes), jnp.bfloat16),
            pltpu.VMEM((2 * windows, src_count, half, lanes), jnp.bfloat16),
            dma((windows, src_count)),
            dma((windows, src_count)),
            dma((2 * windows, rcv_count // 2)),
            dma((2 * windows, rcv_count)),
            dma((2 * windows, rcv_count // 2)),
            dma((windows, rcv_count)),
            dma((windows, rcv_count)),
            dma((2 * windows,)),
            dma((windows,)),
            dma((4,)),
        ],
        compiler_params=pltpu.CompilerParams(
            collective_id=0, has_side_effects=True, vmem_limit_bytes=64 << 20
        ),
        name="spread",
    )(
        raw_samples,
        channel_of_row.reshape(1, rows),
        bin_taper.reshape(1, F),
        jnp.asarray(basis_table(length)),
        live_channels.reshape(1, rows),
    )


def correlate_kernel(pieces, half_index, scale, *refs):
    if half_index:
        own_refs = {1: refs[0]}
        source_ref, *small_refs, left_ref, _, out_ref = refs[1:8]
    else:
        own_refs = dict(enumerate(refs[:2]))
        source_ref, *small_refs, out_ref, left_ref = refs[2:8]
    reach_ref, straight_ref, swapped_ref, small_sem = refs[8:12]
    high_ref, rcv_ref, turned_ref, even_ref, odd_ref = refs[12:]
    step = pl.program_id(0)
    local, src_count, half, lanes = source_ref.shape[1:]
    halves = 2
    windows = pieces * local
    count = src_count * half
    rows = halves * count
    columns = CHUNK * LAGS
    src, rcv = lax.axis_index("src"), lax.axis_index("rcv")

    def rotate(first, target):
        for w in range(windows):
            span = slice(w * lanes, (w + 1) * lanes)
            shape = (CHUNK, GROUP, lanes)
            plain = rcv_ref[pl.ds(first, CHUNK), span]
            turned = turned_ref[pl.ds(first, CHUNK), span]
            plain = jnp.broadcast_to(plain[:, None, :], shape).astype(jnp.bfloat16)
            turned = jnp.broadcast_to(turned[:, None, :], shape).astype(jnp.bfloat16)
            for lag in range(0, LAGS, GROUP):
                straight = straight_ref[lag : lag + GROUP][None]
                swapped = swapped_ref[lag : lag + GROUP][None]
                target[:, lag : lag + GROUP, span] = plain * straight + turned * swapped

    @pl.when(step == 0)
    def _():
        copies = [
            pltpu.make_async_copy(source, target, small_sem.at[n])
            for n, (source, target) in enumerate(
                zip(small_refs, (reach_ref, straight_ref, swapped_ref))
            )
        ]
        for copy in copies:
            copy.start()
        natural = lax.broadcasted_iota(jnp.int32, (count, count), 0)
        held = lax.broadcasted_iota(jnp.int32, (count, count), 1)
        pick = natural == (held % half) * src_count + held // half
        pick = pick.astype(jnp.float32).astype(jnp.bfloat16)
        for d in range(pieces):
            span = slice(d * local * lanes, (d + 1) * local * lanes)
            own = {
                h: jnp.concatenate([ref[d, n].reshape(count, lanes) for n in range(local)], axis=1)
                for h, ref in own_refs.items()
            }
            if not half_index:
                for h in range(halves):
                    left_ref[h * count : (h + 1) * count, span] = jnp.dot(
                        pick, own[h], preferred_element_type=jnp.float32
                    ).astype(jnp.bfloat16)
            other = jnp.concatenate(
                [source_ref[d, n].reshape(count, lanes) for n in range(local)], axis=1
            )
            block = jnp.where(rcv == 0, own[half_index], other)
            value = jnp.dot(pick, block, preferred_element_type=jnp.float32)
            rcv_ref[:, span] = value
            for n in range(local):
                at = (d * local + n) * lanes
                turned_ref[:, at : at + lanes] = pltpu.roll(
                    value[:, n * lanes : (n + 1) * lanes], F, 1
                )
        for copy in copies:
            copy.wait()
        rotate(0, even_ref)
        row = lax.broadcasted_iota(jnp.int32, (rows, rows), 0)
        column = lax.broadcasted_iota(jnp.int32, (rows, rows), 1)
        reach = jnp.where(row == column, reach_ref[...].astype(jnp.float32), 0.0)
        reach = jnp.sum(reach, axis=1, keepdims=True).astype(jnp.int32)
        first = (lax.broadcasted_iota(jnp.int32, (rows, 1), 0) - rcv * rows) * LAGS
        last = first + reach * LAGS + (LAGS - 1)
        high_ref[...] = jnp.where(src + rcv < src_count, last, -1)

    low = (lax.broadcasted_iota(jnp.int32, (rows, 1), 0) - rcv * rows) * LAGS
    high = high_ref[...]

    def multiply(source, turn):
        total = lax.dot_general(
            left_ref[...],
            source[...].reshape(columns, windows * lanes),
            (((1,), (1,)), ((), ())),
            preferred_element_type=jnp.float32,
        )
        column = lax.broadcasted_iota(jnp.int32, (1, columns), 1)
        column = column + (2 * step + turn) * columns + half_index * count * LAGS
        keep = (column >= low) & (column <= high)
        out_ref[:, turn * columns : (turn + 1) * columns] = jnp.where(
            keep, total * scale, 0.0
        ).astype(jnp.bfloat16)

    rotate((2 * step + 1) * CHUNK, odd_ref)
    multiply(even_ref, 0)
    rotate(jnp.minimum(2 * step + 2, count // CHUNK - 1) * CHUNK, even_ref)
    multiply(odd_ref, 1)


def correlate(blocks, receivers, band_reach, length, earlier=None):
    half_index = int(earlier is not None)
    pieces, local, src_count, half, lanes = receivers.shape
    halves = 2
    count = src_count * half
    rows = halves * count
    windows = pieces * local
    depth = windows * lanes
    columns = CHUNK * LAGS
    steps = count // (2 * CHUNK)
    straight, swapped = lag_tables(length)
    whole = lambda *shape: pl.BlockSpec(shape, lambda g: (0,) * len(shape))
    operands = [
        *blocks, receivers, band_reach.reshape(1, rows), jnp.asarray(straight), jnp.asarray(swapped)
    ]
    in_specs = [whole(*operand.shape) for operand in operands]
    in_specs[-3:] = [pl.BlockSpec(memory_space=pltpu.HBM)] * 3
    out_shape = [jax.ShapeDtypeStruct((rows, rows * LAGS), jnp.bfloat16)]
    out_specs = [pl.BlockSpec((rows, 2 * columns), lambda g: (0, g + half_index * steps))]
    aliases = {}
    if half_index:
        operands += [earlier[1], earlier[0]]
        in_specs += [whole(rows, depth), pl.BlockSpec(memory_space=pl.ANY)]
        aliases = {len(operands) - 1: 0}
    else:
        out_shape.append(jax.ShapeDtypeStruct((rows, depth), jnp.bfloat16))
        out_specs.append(whole(rows, depth))
    return pl.pallas_call(
        functools.partial(correlate_kernel, pieces, half_index, 1.0 / math.sqrt(windows)),
        grid=(steps,),
        out_shape=out_shape,
        in_specs=in_specs,
        out_specs=out_specs,
        scratch_shapes=[
            pltpu.VMEM((1, rows), jnp.int32),
            pltpu.VMEM((LAGS, lanes), jnp.bfloat16),
            pltpu.VMEM((LAGS, lanes), jnp.bfloat16),
            pltpu.SemaphoreType.DMA((3,)),
            pltpu.VMEM((rows, 1), jnp.int32),
            pltpu.VMEM((count, depth), jnp.float32),
            pltpu.VMEM((count, depth), jnp.float32),
            pltpu.VMEM((CHUNK, LAGS, depth), jnp.bfloat16),
            pltpu.VMEM((CHUNK, LAGS, depth), jnp.bfloat16),
        ],
        input_output_aliases=aliases,
        cost_estimate=pl.CostEstimate(
            flops=2 * rows * depth * count * LAGS,
            bytes_accessed=2 * rows * count * LAGS,
            transcendentals=0,
        ),
        compiler_params=pltpu.CompilerParams(vmem_limit_bytes=64 << 20),
        name="correlate",
    )(*operands)


def body(raw_samples, channel_of_row, live_channels, band_reach, bin_taper):
    src_count = lax.axis_size("src")
    rcv_count = lax.axis_size("rcv")
    length = raw_samples.shape[2]
    first, second, near = spread(
        raw_samples, channel_of_row, live_channels, bin_taper, src_count, rcv_count
    )
    route = []
    for s in range(src_count):
        for to in range(1, rcv_count):
            if s >= to:
                holder = to if to < 3 or to % 2 == 0 else (to - 2 if to > 3 else 0)
                route.append((s * rcv_count + holder, (s - to) * rcv_count + to))
    far = lax.ppermute(second, ("src", "rcv"), route)
    earlier = correlate([first, second], near, band_reach, length)
    return correlate([second], far, band_reach, length, earlier)[0]


def solution(mesh):
    return jax.shard_map(
        body,
        mesh=mesh,
        in_specs=(P("rcv", "src", None), P("src"), P("src"), P("src"), P()),
        out_specs=P("src", "rcv"),
        check_vma=False,
    )
```
